32 devices in a mesh: grp: 8 (over z, x), uly: 4 (over y, core).
Axes of the slice: x: 2, y: 2, z: 4, core: 2. Of those that a mesh axis runs over, the one named last changes fastest.
Arguments:
- tokens: bfloat16 [4096, 3072], P(('grp', 'uly')), may hold values from -60 to 60
- block_image: int32 [512], P(('grp', 'uly')), may hold values from 0 to 15, as said below
- dest_slot: int32 [512], P(('grp', 'uly')), may hold values from 0 to 15, as said below
- timestep: int32 [16], P('grp'), may hold values from 0 to 999
- txt_len: int32 [16], P('grp'), may hold values from 1 to 128
- mod_weight: bfloat16 [256, 9216], replicated, may hold values from -0.375 to 0.375
- qkv_weight: bfloat16 [3072, 6144], P('grp', 'uly'), may hold values from -0.109375 to 0.109375
- q_gain: float32 [128], replicated, may hold values from 1 to 2.5
- k_gain: float32 [128], replicated, may hold values from 1 to 2.5
- text_kv: bfloat16 [16, 128, 4096], P('grp', None, 'uly'), may hold values from -6 to 6
- out_weight: bfloat16 [2048, 3072], P(None, 'grp'), may hold values from -0.125 to 0.125
Outputs:
- update: bfloat16 [4096, 3072], P(('grp', 'uly'))
The draws below stay inside these ranges and needn't reach their ends.
Inputs may be any that keep to these rules, and one draw needn't show every extreme that they name: `block_image`: image i belongs to group i // 2, and every image has at least 256 tokens. The blocks of one device name images of any one group at most 2 times, and some device does so 2 times. `dest_slot`: A block keeps its uly index and goes to group block_image // 2; every block slot of every device receives exactly one block. Along a group's positions, uly index times 16 plus slot, each image's blocks are contiguous and images come in increasing order.
All inputs are finite; a program needn't handle non-finite values.
Results may differ from the reference program's by a relative error of at most 0.015.
Values may be sent and summed in bfloat16 or wider, within the bound.
A program may use at most 128 MiB of HBM per device.

```python
import math
import jax
import jax.numpy as jnp
from jax import lax

D = 3072
HEADS = 16
HD = 128
TEMB = 256
TXT = 128
BLK = 8
MIN_TOK = 256
IMG_GRP = 2
BLK_DEV = 16
GTOK = 512
IMAGES = 16
BLOCKS = 512
TOKENS = 4096
N_GRP = 8
N_ULY = 4


def plan_tables(key):
    groups = N_GRP
    columns = N_ULY
    per_device = BLK_DEV
    per_group = per_device * columns
    least = MIN_TOK // BLK
    extra = per_group - IMG_GRP * least
    units = max(extra, 1)
    key_len, key_col = jax.random.split(jax.random.fold_in(key, 101))
    weights = jax.random.randint(jax.random.fold_in(key_len, 1), (groups, IMG_GRP), 1, 9)
    cumulative = jnp.cumsum(weights, axis=1)
    picks = jax.random.randint(jax.random.fold_in(key_len, 2), (groups, units), 0, cumulative[:, -1:])
    chosen = jnp.sum(picks[:, :, None] >= cumulative[:, None, :], axis=2)
    live = (jnp.arange(units) < extra).astype(jnp.int32)
    counts = jnp.sum((chosen[:, :, None] == jnp.arange(IMG_GRP)[None, None, :]).astype(jnp.int32) * live[None, :, None], axis=1)
    lengths = least + counts
    ends = jnp.cumsum(lengths, axis=1)
    positions = jnp.arange(per_group)
    image_at = jnp.sum(positions[None, :, None] >= ends[:, None, :], axis=2).astype(jnp.int32)

    def column(ckey):
        key_a, key_b, key_c, key_d = jax.random.split(ckey, 4)
        first = jax.random.permutation(key_a, groups)
        second = jax.random.permutation(key_b, groups)
        base = per_device // groups
        rest = per_device % groups
        table = base + ((first[:, None] + second[None, :]) % groups < rest).astype(jnp.int32)
        running = jnp.cumsum(table, axis=1)
        order = jnp.arange(per_device)
        ordered = jnp.sum(order[None, :, None] >= running[:, None, :], axis=2)
        shuffles = jax.vmap(lambda k: jax.random.permutation(k, per_device))(jax.random.split(key_c, groups))
        target = jnp.take_along_axis(ordered, shuffles, axis=1)
        flat = target.reshape(-1)
        hits = (flat[:, None] == jnp.arange(groups)[None, :]).astype(jnp.int32)
        rank = jnp.sum((jnp.cumsum(hits, axis=0) - hits) * hits, axis=1)
        spots = jax.vmap(lambda k: jax.random.permutation(k, per_device))(jax.random.split(key_d, groups))
        slot = spots[flat, rank].reshape(groups, per_device)
        return (target, slot)
    target, slot = jax.vmap(column)(jax.random.split(key_col, columns))
    target = target.transpose(1, 0, 2)
    slot = slot.transpose(1, 0, 2)
    spot = jnp.arange(columns)[None, :, None] * per_device + slot
    image = target * IMG_GRP + image_at[target, spot]
    return (image.reshape(-1).astype(jnp.int32), slot.reshape(-1).astype(jnp.int32))


def draw_block_image(key, part):
    shared = plan_tables(key)
    return shared[0]


def draw_dest_slot(key, part):
    shared = plan_tables(key)
    return shared[1]


def draw_txt_len(key, part):
    key = jax.random.fold_in(key, 5)
    key_a, key_b = jax.random.split(key)
    lens = jax.random.randint(key_a, (IMAGES,), 1, TXT + 1)
    where = jax.random.randint(key_b, (), 0, IMAGES)
    lens = lens.at[where].set(TXT)
    lens = lens.at[(where + 1) % IMAGES].set(1)
    return lens.astype(jnp.int32)


def draw_tokens(key, part):
    key = jax.random.fold_in(key, 3)
    key_a = jax.random.fold_in(key, 0)
    base = jax.random.normal(key_a, (TOKENS, D), jnp.float32)
    values = jnp.clip(base, -6.0, 6.0)
    return values.astype(jnp.bfloat16)


def plant(array, rng, low, top_value):
    extent = array.shape
    place = [jax.random.randint(jax.random.fold_in(rng, axis), (), 0, extent[axis]) for axis in range(len(extent))]
    array = array.at[tuple(place)].set(low)
    longest = extent.index(max(extent))
    place[longest] = (place[longest] + 1) % extent[longest]
    return array.at[tuple(place)].set(top_value)


def level_of(key, dims, cuts, low, high):
    level = 1.0
    for dim, shards_of in cuts:
        draws = jax.random.uniform(jax.random.fold_in(jax.random.fold_in(key, 6), dim), (shards_of,), jnp.float32, low / len(cuts), high / len(cuts))
        level = level * jnp.repeat(jnp.exp(draws), dims[dim] // shards_of).reshape((-1,) + (1,) * (len(dims) - 1 - dim))
    return level


def gaussian(own_key, extent, width, bound, cuts=(), kind=jnp.bfloat16):
    values = jax.random.normal(own_key, extent, jnp.float32) * width
    if len(cuts) > 0:
        values = level_of(own_key, extent, cuts, -0.22, 0.18) * values
    return jnp.clip(values, min=-bound, max=bound).astype(kind)


def setup_inputs(seed: int = 0) -> dict:
    splits = jax.random.split(jax.random.key(seed), 12)
    return {
        "tokens": draw_tokens(jax.random.fold_in(splits[11], 71), 0),
        "block_image": draw_block_image(jax.random.fold_in(splits[11], 71), 0),
        "dest_slot": draw_dest_slot(jax.random.fold_in(splits[11], 71), 0),
        "timestep": plant(jax.random.randint(splits[3], (IMAGES,), 0, 1000), jax.random.fold_in(splits[3], 1), 0, 999).astype(jnp.int32),
        "txt_len": draw_txt_len(jax.random.fold_in(splits[11], 71), 0),
        "mod_weight": gaussian(splits[5], (TEMB, 3 * D), TEMB ** -0.5, 0.375),
        "qkv_weight": gaussian(splits[6], (D, 3 * HEADS * HD), D ** -0.5, 0.109375, ((0, 8), (1, 4))),
        "q_gain": jnp.clip(jnp.exp(jax.random.uniform(splits[7], (HD,), jnp.float32, math.log(1.0), math.log(2.5))), 1.0, 2.5),
        "k_gain": jnp.clip(jnp.exp(jax.random.uniform(splits[8], (HD,), jnp.float32, math.log(1.0), math.log(2.5))), 1.0, 2.5),
        "text_kv": gaussian(splits[9], (IMAGES, TXT, 2 * HEADS * HD), 1.0, 6.0, ((0, 8), (2, 4))),
        "out_weight": gaussian(splits[10], (HEADS * HD, D), (HEADS * HD) ** -0.5, 0.125, ((1, 8),)),
    }


def layer_norm(values):
    mean = lax.optimization_barrier(jnp.mean(values, axis=-1, keepdims=True))
    centred = values - mean
    spread = lax.optimization_barrier(jnp.mean(centred * centred, axis=-1, keepdims=True))
    return centred * lax.rsqrt(spread + 1e-06)

def rms_scale(values, gain):
    return values * lax.rsqrt(lax.optimization_barrier(jnp.mean(values * values, axis=-1, keepdims=True)) + 1e-06) * gain

def modulation(timestep, mod_weight):
    half = mod_weight.shape[0] // 2
    freqs = jnp.exp(-math.log(10000.0) * jnp.arange(half, dtype=jnp.float32) / half)
    angles = timestep.astype(jnp.float32)[:, None] * freqs[None, :]
    embedded = jnp.concatenate([jnp.cos(angles), jnp.sin(angles)], axis=1)
    active = jax.nn.silu(embedded).astype(jnp.bfloat16)
    return jnp.dot(active, mod_weight, preferred_element_type=jnp.float32)

def select_rows(mods, owner):
    onehot = (owner[:, None] == jnp.arange(mods.shape[0], dtype=jnp.int32)[None, :]).astype(jnp.float32)
    return jnp.dot(onehot, mods, precision=lax.Precision.HIGHEST)

def head_attention(query, keys, values, q_owner, k_owner, k_live):
    scores = jnp.dot(query, keys.T, preferred_element_type=jnp.float32) * query.shape[-1] ** (-0.5)
    match = (q_owner[:, None] == k_owner[None, :]) & k_live[None, :]
    weights = jnp.where(match, jnp.exp(scores), 0.0)
    total = lax.optimization_barrier(jnp.sum(weights, axis=1, keepdims=True))
    summed = jnp.dot(weights.astype(jnp.bfloat16), values, preferred_element_type=jnp.float32)
    return (summed / total).astype(jnp.bfloat16)

def reference(tokens, block_image, dest_slot, timestep, txt_len, mod_weight, qkv_weight, q_gain, k_gain, text_kv, out_weight):
    images = block_image.reshape(N_GRP, N_ULY, BLK_DEV)
    slots = dest_slot.reshape(N_GRP, N_ULY, BLK_DEV)
    column = jnp.arange(N_ULY, dtype=jnp.int32)[None, :, None]
    target = (images // IMG_GRP * N_ULY + column) * BLK_DEV + slots
    target = target.reshape(-1).astype(jnp.int32)
    blocks = tokens.reshape(BLOCKS, BLK, D)
    moved = jnp.zeros_like(blocks).at[target].set(blocks).reshape(N_GRP, GTOK, D)
    owners = jnp.zeros((BLOCKS,), jnp.int32).at[target].set(images.reshape(-1) % IMG_GRP)
    owners = owners.reshape(N_GRP, BLK_DEV * N_ULY)

    def one_group(pack):
        rows, owner_blocks, steps_here, lens_here, text_here = pack
        mods = modulation(steps_here, mod_weight)
        owner = jnp.repeat(owner_blocks, BLK)
        picked = select_rows(mods, owner)
        shift = picked[:, :D]
        scale = picked[:, D:2 * D]
        gate = picked[:, 2 * D:]
        hidden = (layer_norm(rows.astype(jnp.float32)) * (1.0 + scale) + shift).astype(jnp.bfloat16)
        projected = jnp.dot(hidden, qkv_weight, preferred_element_type=jnp.float32).reshape(-1, HEADS, 3, HD)
        query = rms_scale(projected[:, :, 0], q_gain).astype(jnp.bfloat16)
        keys = rms_scale(projected[:, :, 1], k_gain).astype(jnp.bfloat16)
        values = projected[:, :, 2].astype(jnp.bfloat16)
        text = text_here.reshape(IMG_GRP, TXT, HEADS, 2, HD)
        text_key = rms_scale(text[:, :, :, 0].astype(jnp.float32), k_gain).astype(jnp.bfloat16)
        text_key = text_key.reshape(IMG_GRP * TXT, HEADS, HD)
        text_value = text[:, :, :, 1].reshape(IMG_GRP * TXT, HEADS, HD)
        all_keys = jnp.concatenate([keys, text_key], axis=0)
        all_values = jnp.concatenate([values, text_value], axis=0)
        text_owner = jnp.repeat(jnp.arange(IMG_GRP, dtype=jnp.int32), TXT)
        text_live = jnp.tile(jnp.arange(TXT, dtype=jnp.int32), IMG_GRP) < jnp.repeat(lens_here, TXT)
        k_owner = jnp.concatenate([owner, text_owner])
        k_live = jnp.concatenate([jnp.ones(owner.shape, bool), text_live])

        def per_head(trio):
            return head_attention(trio[0], trio[1], trio[2], owner, k_owner, k_live)
        mixed = lax.map(per_head, (query.transpose(1, 0, 2), all_keys.transpose(1, 0, 2), all_values.transpose(1, 0, 2)))
        mixed = mixed.transpose(1, 0, 2).reshape(-1, HEADS * HD)
        projection = jnp.dot(mixed, out_weight, preferred_element_type=jnp.float32)
        return (gate * projection).astype(jnp.bfloat16)
    result = lax.map(one_group, (moved, owners, timestep.reshape(N_GRP, IMG_GRP), txt_len.reshape(N_GRP, IMG_GRP), text_kv.reshape(N_GRP, IMG_GRP, TXT, 2 * HEADS * HD)))
    return result.reshape(TOKENS, D)
```

```python
import functools
import math

import jax
import jax.numpy as jnp
from jax import lax
from jax.experimental import pallas as pl
from jax.experimental.pallas import tpu as pltpu
from jax.sharding import PartitionSpec as P

HD = 128
TXT = 128
BLK = 8
IMG_GRP = 2


def layer_norm(values):
    mean = jnp.mean(values, axis=-1, keepdims=True)
    centred = values - mean
    spread = jnp.mean(centred * centred, axis=-1, keepdims=True)
    return centred * lax.rsqrt(spread + 1e-06)


def rms_scale(values, gain):
    return values * lax.rsqrt(jnp.mean(values * values, axis=-1, keepdims=True) + 1e-06) * gain


def modulation(timestep, mod_weight):
    half = mod_weight.shape[0] // 2
    freqs = jnp.exp(-math.log(10000.0) * jnp.arange(half, dtype=jnp.float32) / half)
    angles = timestep.astype(jnp.float32)[:, None] * freqs[None, :]
    embedded = jnp.concatenate([jnp.cos(angles), jnp.sin(angles)], axis=1)
    active = jax.nn.silu(embedded).astype(jnp.bfloat16)
    return jnp.dot(active, mod_weight, preferred_element_type=jnp.float32)


def select_rows(mods, owner):
    onehot = (owner[:, None] == jnp.arange(mods.shape[0], dtype=jnp.int32)[None, :]).astype(
        jnp.float32
    )
    return jnp.dot(onehot, mods, precision=lax.Precision.HIGHEST)


def tile_terms(query, q_owner, keys, values, k_owner, k_live):
    scores = jnp.einsum(
        "qhd,khd->hqk", query, keys, preferred_element_type=jnp.float32
    ) * query.shape[-1] ** (-0.5)
    match = (q_owner[:, None] == k_owner[None, :]) & k_live[None, :]
    weights = jnp.where(match[None], jnp.exp(scores), 0.0)
    total = jnp.sum(weights, axis=2)
    summed = jnp.einsum(
        "hqk,khd->qhd", weights.astype(jnp.bfloat16), values, preferred_element_type=jnp.float32
    )
    return (total, summed)


MESH = pl.DeviceIdType.MESH
CHUNKS = 2


def fused_kernel(
    groups,
    lanes,
    pad,
    tokens_ref,
    place_ref,
    tags_ref,
    mods_ref,
    weight_ref,
    acc_ref,
    count_ref,
    out_blocks,
    in_blocks,
    in_tags,
    hidden_all,
    weight_all,
    counts_all,
    block_send,
    block_recv,
    tag_send,
    tag_recv,
    hid_send,
    hid_recv,
    cnt_send,
    cnt_recv,
    ring_send,
    ring_recv,
):
    g = lax.axis_index("grp")
    u = lax.axis_index("uly")
    rows, width = tokens_ref.shape
    depth, columns = weight_ref.shape
    half = columns // 2
    piece = depth // CHUNKS
    span = groups * pad

    def group_at(position):
        high = position // (groups // 2)
        return (1 - high) * 2 * position + high * (2 * (groups - 1 - position) + 1)

    odd = g % 2
    position = (1 - odd) * (g // 2) + odd * (groups - 1 - g // 2)
    ahead = group_at((position + 1) % groups)
    behind = group_at((position + groups - 1) % groups)

    barrier = pltpu.get_barrier_semaphore()
    for k in range(1, groups):
        pl.semaphore_signal(
            barrier, inc=1, device_id=((g + k) % groups, u), device_id_type=MESH
        )
    for k in range(1, lanes):
        pl.semaphore_signal(barrier, inc=1, device_id=(g, (u + k) % lanes), device_id_type=MESH)

    spot = lax.broadcasted_iota(jnp.int32, (span, rows), 0)
    pick = jnp.where(spot == place_ref[0:1, :], 1.0, 0.0).astype(jnp.bfloat16)
    sorted_rows = jnp.dot(pick, tokens_ref[...], preferred_element_type=jnp.float32)
    out_blocks[...] = sorted_rows.astype(jnp.bfloat16).reshape(groups, pad, width)
    in_blocks[g] = out_blocks[g]
    in_tags[g] = tags_ref[g]

    pl.semaphore_wait(barrier, groups + lanes - 2)

    def ring_copy(way, chunk, step):
        if way == 0:
            owner = group_at((position + groups - step) % groups)
            target = ahead
        else:
            owner = group_at((position + step) % groups)
            target = behind
        place = weight_all.at[
            owner, pl.ds(chunk * piece, piece), pl.ds(way * half, half)
        ]
        return pltpu.make_async_remote_copy(
            src_ref=place,
            dst_ref=place,
            send_sem=ring_send.at[way, chunk, step],
            recv_sem=ring_recv.at[way, chunk, step],
            device_id=(target, u),
            device_id_type=MESH,
        )

    def block_copy(k):
        peer = (g + k) % groups
        return pltpu.make_async_remote_copy(
            src_ref=out_blocks.at[peer],
            dst_ref=in_blocks.at[g],
            send_sem=block_send.at[k],
            recv_sem=block_recv.at[k],
            device_id=(peer, u),
            device_id_type=MESH,
        )

    def tag_copy(k):
        peer = (g + k) % groups
        return pltpu.make_async_remote_copy(
            src_ref=tags_ref.at[peer],
            dst_ref=in_tags.at[g],
            send_sem=tag_send.at[k],
            recv_sem=tag_recv.at[k],
            device_id=(peer, u),
            device_id_type=MESH,
        )

    for k in range(1, groups):
        tag_copy(k).start()
        block_copy(k).start()
    weight_all[g] = weight_ref[...]
    for chunk in range(CHUNKS):
        for way in range(2):
            ring_copy(way, chunk, 0).start()
    for k in range(1, groups):
        tag_copy(k).wait()
        block_copy(k).wait()

    tag = jnp.max(in_tags[...], axis=0)[0:1, :]
    slot = lax.broadcasted_iota(jnp.int32, (rows, span), 0)
    match = slot == (tag >> 1)
    owner_col = jnp.sum(
        jnp.where(match, (tag & 1).astype(jnp.float32), 0.0), axis=1, keepdims=True
    )
    values = jnp.dot(
        jnp.where(match, 1.0, 0.0).astype(jnp.bfloat16),
        in_blocks[...].reshape(span, width),
        preferred_element_type=jnp.float32,
    )
    mods = mods_ref[...]
    first = owner_col < 0.5
    shift = jnp.where(first, mods[0:1, :width], mods[1:2, :width])
    scale = jnp.where(first, mods[0:1, width : 2 * width], mods[1:2, width : 2 * width])
    hidden = (layer_norm(values) * (1.0 + scale) + shift).astype(jnp.bfloat16)
    mine = pl.ds(pl.multiple_of(u * rows, rows), rows)
    for part in range(groups):
        hidden_all[part, mine, :] = hidden[:, part * depth : (part + 1) * depth]
    counts_all[u] = jnp.broadcast_to(
        jnp.sum(jnp.where(first, 1.0, 0.0), axis=0, keepdims=True), counts_all.shape[1:]
    )

    def hidden_copy(k):
        return pltpu.make_async_remote_copy(
            src_ref=hidden_all.at[:, mine, :],
            dst_ref=hidden_all.at[:, mine, :],
            send_sem=hid_send.at[k],
            recv_sem=hid_recv.at[k],
            device_id=(g, (u + k) % lanes),
            device_id_type=MESH,
        )

    def count_copy(k):
        return pltpu.make_async_remote_copy(
            src_ref=counts_all.at[u],
            dst_ref=counts_all.at[u],
            send_sem=cnt_send.at[k],
            recv_sem=cnt_recv.at[k],
            device_id=(g, (u + k) % lanes),
            device_id_type=MESH,
        )

    for k in range(1, lanes):
        hidden_copy(k).start()
        count_copy(k).start()

    def pass_on(step):
        for chunk in range(CHUNKS):
            for way in range(2):
                ring_copy(way, chunk, step).wait()

                @pl.when(step < groups - 2)
                def _():
                    ring_copy(way, chunk, step + 1).start()

    def add_block(step):
        left = group_at((position + groups - step) % groups)
        right = group_at((position + step) % groups)
        acc_ref[:, :half] += jnp.dot(
            hidden_all[left], weight_all[left, :, :half], preferred_element_type=jnp.float32
        )
        acc_ref[:, half:] += jnp.dot(
            hidden_all[right], weight_all[right, :, half:], preferred_element_type=jnp.float32
        )

    early = groups // 2 - 1

    def forward_only(step, carry):
        pass_on(step)
        return carry

    lax.fori_loop(0, early, forward_only, 0)
    acc_ref[...] = jnp.zeros_like(acc_ref)
    for k in range(1, lanes):
        hidden_copy(k).wait()
        count_copy(k).wait()
    count_ref[...] = jnp.sum(counts_all[...], axis=0)

    def held(step, carry):
        add_block(step)
        return carry

    def arriving(step, carry):
        pass_on(step)
        add_block(step + 1)
        return carry

    lax.fori_loop(0, early + 1, held, 0)
    lax.fori_loop(early, groups - 1, arriving, 0)


def project(tokens, place, tags, mods, qkv_weight, pad):
    groups = lax.axis_size("grp")
    lanes = lax.axis_size("uly")
    rows, width = tokens.shape
    depth, columns = qkv_weight.shape
    vmem = pl.BlockSpec(memory_space=pltpu.VMEM)
    dma = pltpu.SemaphoreType.DMA
    return pl.pallas_call(
        functools.partial(fused_kernel, groups, lanes, pad),
        out_shape=(
            jax.ShapeDtypeStruct((rows * lanes, columns), jnp.float32),
            jax.ShapeDtypeStruct((8, 128), jnp.float32),
        ),
        in_specs=[vmem] * 5,
        out_specs=(vmem, vmem),
        scratch_shapes=[
            pltpu.VMEM((groups, pad, width), jnp.bfloat16),
            pltpu.VMEM((groups, pad, width), jnp.bfloat16),
            pltpu.VMEM((groups, 8, groups * pad), jnp.int32),
            pltpu.VMEM((groups, rows * lanes, depth), jnp.bfloat16),
            pltpu.VMEM((groups, depth, columns), jnp.bfloat16),
            pltpu.VMEM((lanes, 8, 128), jnp.float32),
            dma((groups,)),
            dma((groups,)),
            dma((groups,)),
            dma((groups,)),
            dma((lanes,)),
            dma((lanes,)),
            dma((lanes,)),
            dma((lanes,)),
            dma((2, CHUNKS, groups)),
            dma((2, CHUNKS, groups)),
        ],
        compiler_params=pltpu.CompilerParams(
            collective_id=0, has_side_effects=True, vmem_limit_bytes=48 * 1024 * 1024
        ),
        cost_estimate=pl.CostEstimate(
            flops=2 * rows * lanes * width * columns,
            bytes_accessed=200 * 1024 * 1024,
            transcendentals=0,
        ),
    )(tokens, place, tags, mods, qkv_weight)


def output_kernel(lanes, mixed_ref, weight_ref, out_ref, sending, landing, send_sem, recv_sem):
    g = lax.axis_index("grp")
    u = lax.axis_index("uly")
    rows = out_ref.shape[0]
    barrier = pltpu.get_barrier_semaphore()
    for k in range(1, lanes):
        pl.semaphore_signal(barrier, inc=1, device_id=(g, (u + k) % lanes), device_id_type=MESH)
    pl.semaphore_wait(barrier, lanes - 1)

    def part(index):
        return jnp.dot(
            mixed_ref[pl.ds(pl.multiple_of(index * rows, rows), rows), :],
            weight_ref[...],
            preferred_element_type=jnp.float32,
        )

    def copy(k):
        return pltpu.make_async_remote_copy(
            src_ref=sending.at[k - 1],
            dst_ref=landing.at[k - 1],
            send_sem=send_sem.at[k - 1],
            recv_sem=recv_sem.at[k - 1],
            device_id=(g, (u + k) % lanes),
            device_id_type=MESH,
        )

    order = sorted(range(1, lanes), key=lambda k: abs(k - lanes // 2))
    for k in order:
        sending[k - 1] = part((u + k) % lanes).astype(jnp.bfloat16)
        copy(k).start()
    out_ref[...] = part(u)
    for k in order:
        copy(k).wait()
        out_ref[...] += landing[k - 1].astype(jnp.float32)


def output_projection(mixed, weight):
    lanes = lax.axis_size("uly")
    rows = mixed.shape[0] // lanes
    width = weight.shape[1]
    vmem = pl.BlockSpec(memory_space=pltpu.VMEM)
    return pl.pallas_call(
        functools.partial(output_kernel, lanes),
        out_shape=jax.ShapeDtypeStruct((rows, width), jnp.float32),
        in_specs=[vmem] * 2,
        out_specs=vmem,
        scratch_shapes=[
            pltpu.VMEM((lanes - 1, rows, width), jnp.bfloat16),
            pltpu.VMEM((lanes - 1, rows, width), jnp.bfloat16),
            pltpu.SemaphoreType.DMA((lanes - 1,)),
            pltpu.SemaphoreType.DMA((lanes - 1,)),
        ],
        compiler_params=pltpu.CompilerParams(
            collective_id=1, has_side_effects=True, vmem_limit_bytes=40 * 1024 * 1024
        ),
    )(mixed, weight)


def body(
    tokens,
    block_image,
    dest_slot,
    timestep,
    txt_len,
    mod_weight,
    qkv_weight,
    q_gain,
    k_gain,
    text_kv,
    out_weight,
):
    groups = lax.axis_size("grp")
    lanes = lax.axis_size("uly")
    rows, width = tokens.shape
    blocks = block_image.shape[0]
    capacity = (blocks + groups - 1) // groups
    pad = (capacity * BLK + 15) // 16 * 16
    span = groups * pad
    g = lax.axis_index("grp")
    u = lax.axis_index("uly")
    target = block_image // IMG_GRP
    own_image = block_image % IMG_GRP
    index = jnp.arange(blocks, dtype=jnp.int32)
    before = jnp.sum(
        ((target[:, None] == target[None, :]) & (index[None, :] < index[:, None])).astype(jnp.int32),
        axis=1,
    )
    row = jnp.arange(BLK, dtype=jnp.int32)
    place = ((target * pad + before * BLK)[:, None] + row[None, :]).reshape(rows)
    code = ((dest_slot[:, None] * BLK + row[None, :]) * 2 + own_image[:, None]).reshape(rows)
    hits = place[None, :] == jnp.arange(span, dtype=jnp.int32)[:, None]
    codes = (jnp.sum(jnp.where(hits, code[None, :] + 1, 0), axis=1) - 1).reshape(groups, pad)
    own_lane = jnp.arange(span, dtype=jnp.int32) // pad == g
    tags = jnp.where(own_lane[None, :], jnp.tile(codes, (1, groups)), -1)
    tags = jnp.broadcast_to(tags[:, None, :], (groups, 8, span))
    places = jnp.broadcast_to(place[None, :], (8, rows))

    share = out_weight.shape[0] // lanes
    own_rows = lax.dynamic_slice_in_dim(out_weight, u * share, share, axis=0)
    out_rows = lax.all_gather(own_rows, "grp", axis=1, tiled=True)

    mods = modulation(timestep, mod_weight)
    projected, count = project(tokens, places, tags, mods, qkv_weight, pad)
    local_heads = qkv_weight.shape[1] // (3 * HD)
    group_tokens = rows * lanes
    projected = projected.reshape(-1, local_heads, 3, HD)
    query = rms_scale(projected[:, :, 0], q_gain).astype(jnp.bfloat16)
    keys = rms_scale(projected[:, :, 1], k_gain).astype(jnp.bfloat16)
    values = projected[:, :, 2].astype(jnp.bfloat16)
    text = text_kv.reshape(IMG_GRP, TXT, local_heads, 2, HD)
    text_key = (
        rms_scale(text[:, :, :, 0].astype(jnp.float32), k_gain)
        .astype(jnp.bfloat16)
        .reshape(IMG_GRP * TXT, local_heads, HD)
    )
    text_value = text[:, :, :, 1].reshape(IMG_GRP * TXT, local_heads, HD)
    first_count = count[0, 0].astype(jnp.int32)
    owner = (jnp.arange(group_tokens, dtype=jnp.int32) >= first_count).astype(jnp.int32)
    text_owner = jnp.repeat(jnp.arange(IMG_GRP, dtype=jnp.int32), TXT)
    text_live = jnp.tile(jnp.arange(TXT, dtype=jnp.int32), IMG_GRP) < jnp.repeat(txt_len, TXT)
    all_keys = jnp.concatenate([keys, text_key], axis=0)
    all_values = jnp.concatenate([values, text_value], axis=0)
    k_owner = jnp.concatenate([owner, text_owner])
    k_live = jnp.concatenate([jnp.ones(owner.shape, bool), text_live])
    total, summed = tile_terms(query, owner, all_keys, all_values, k_owner, k_live)
    mixed = (summed / total.T[:, :, None]).astype(jnp.bfloat16)
    mixed = mixed.reshape(group_tokens, local_heads * HD)
    projection = output_projection(mixed, out_rows)
    own_first = (u * rows + jnp.arange(rows, dtype=jnp.int32)) < first_count
    gate = jnp.where(own_first[:, None], mods[0:1, 2 * width :], mods[1:2, 2 * width :])
    return (gate * projection).astype(jnp.bfloat16)


def solution(mesh):
    return jax.shard_map(
        body,
        mesh=mesh,
        in_specs=(
            P(("grp", "uly"), None),
            P(("grp", "uly")),
            P(("grp", "uly")),
            P("grp"),
            P("grp"),
            P(),
            P("grp", "uly"),
            P(),
            P(),
            P("grp", None, "uly"),
            P(None, "grp"),
        ),
        out_specs=P(("grp", "uly"), None),
        check_vma=False,
    )
```

```python
import functools
import math

import jax
import jax.numpy as jnp
from jax import lax
from jax.experimental import pallas as pl
from jax.experimental.pallas import tpu as pltpu
from jax.sharding import PartitionSpec as P

HD = 128
TXT = 128
BLK = 8
IMG_GRP = 2


def layer_norm(values):
    mean = jnp.mean(values, axis=-1, keepdims=True)
    centred = values - mean
    spread = jnp.mean(centred * centred, axis=-1, keepdims=True)
    return centred * lax.rsqrt(spread + 1e-06)


def rms_scale(values, gain):
    return values * lax.rsqrt(jnp.mean(values * values, axis=-1, keepdims=True) + 1e-06) * gain


def modulation(timestep, mod_weight):
    half = mod_weight.shape[0] // 2
    freqs = jnp.exp(-math.log(10000.0) * jnp.arange(half, dtype=jnp.float32) / half)
    angles = timestep.astype(jnp.float32)[:, None] * freqs[None, :]
    embedded = jnp.concatenate([jnp.cos(angles), jnp.sin(angles)], axis=1)
    active = jax.nn.silu(embedded).astype(jnp.bfloat16)
    return jnp.dot(active, mod_weight, preferred_element_type=jnp.float32)


MESH = pl.DeviceIdType.MESH
CHUNKS = 2


def fused_kernel(
    groups,
    lanes,
    pad,
    tokens_ref,
    place_ref,
    tags_ref,
    mods_ref,
    weight_ref,
    gains_ref,
    text_ref,
    text_code_ref,
    out_weight_ref,
    out_ref,
    acc_ref,
    out_weight_all,
    text_keys,
    mixed_ref,
    own_sum,
    sending,
    landing,
    out_blocks,
    in_blocks,
    in_tags,
    hidden_all,
    weight_all,
    counts_all,
    block_send,
    block_recv,
    tag_send,
    tag_recv,
    hid_send,
    hid_recv,
    cnt_send,
    cnt_recv,
    ring_send,
    ring_recv,
    out_send,
    out_recv,
    sum_send,
    sum_recv,
    local_sem,
):
    g = lax.axis_index("grp")
    u = lax.axis_index("uly")
    rows, width = tokens_ref.shape
    depth, columns = weight_ref.shape
    half = columns // 2
    piece = depth // CHUNKS
    span = groups * pad
    share = out_weight_all.shape[1]
    out_piece = share // CHUNKS
    heads = columns // (3 * HD)
    count = rows * lanes

    def group_at(position):
        high = position // (groups // 2)
        return (1 - high) * 2 * position + high * (2 * (groups - 1 - position) + 1)

    odd = g % 2
    position = (1 - odd) * (g // 2) + odd * (groups - 1 - g // 2)
    ahead = group_at((position + 1) % groups)
    behind = group_at((position + groups - 1) % groups)

    own_copy = pltpu.make_async_copy(
        out_weight_ref.at[pl.ds(pl.multiple_of(u * share, share), share), :],
        out_weight_all.at[g],
        local_sem,
    )
    own_copy.start()
    barrier = pltpu.get_barrier_semaphore()
    for k in range(1, groups):
        pl.semaphore_signal(
            barrier, inc=1, device_id=((g + k) % groups, u), device_id_type=MESH
        )
    for k in range(1, lanes):
        pl.semaphore_signal(barrier, inc=1, device_id=(g, (u + k) % lanes), device_id_type=MESH)

    spot = lax.broadcasted_iota(jnp.int32, (span, rows), 0)
    pick = jnp.where(spot == place_ref[0:1, :], 1.0, 0.0).astype(jnp.bfloat16)
    sorted_rows = jnp.dot(pick, tokens_ref[...], preferred_element_type=jnp.float32)
    out_blocks[...] = sorted_rows.astype(jnp.bfloat16).reshape(groups, pad, width)
    in_blocks[g] = out_blocks[g]
    in_tags[g] = tags_ref[g]

    pl.semaphore_wait(barrier, groups + lanes - 2)

    def ring_copy(way, chunk, step):
        if way == 0:
            owner = group_at((position + groups - step) % groups)
            target = ahead
        else:
            owner = group_at((position + step) % groups)
            target = behind
        place = weight_all.at[
            owner, pl.ds(chunk * piece, piece), pl.ds(way * half, half)
        ]
        return pltpu.make_async_remote_copy(
            src_ref=place,
            dst_ref=place,
            send_sem=ring_send.at[way, chunk, step],
            recv_sem=ring_recv.at[way, chunk, step],
            device_id=(target, u),
            device_id_type=MESH,
        )

    def block_copy(k):
        peer = (g + k) % groups
        return pltpu.make_async_remote_copy(
            src_ref=out_blocks.at[peer],
            dst_ref=in_blocks.at[g],
            send_sem=block_send.at[k],
            recv_sem=block_recv.at[k],
            device_id=(peer, u),
            device_id_type=MESH,
        )

    def tag_copy(k):
        peer = (g + k) % groups
        return pltpu.make_async_remote_copy(
            src_ref=tags_ref.at[peer],
            dst_ref=in_tags.at[g],
            send_sem=tag_send.at[k],
            recv_sem=tag_recv.at[k],
            device_id=(peer, u),
            device_id_type=MESH,
        )

    for k in range(1, groups):
        tag_copy(k).start()
        block_copy(k).start()
    weight_all[g] = weight_ref[...]
    for chunk in range(CHUNKS):
        for way in range(2):
            ring_copy(way, chunk, 0).start()
    for k in range(1, groups):
        tag_copy(k).wait()
        block_copy(k).wait()

    tag = jnp.max(in_tags[...], axis=0)[0:1, :]
    slot = lax.broadcasted_iota(jnp.int32, (rows, span), 0)
    match = slot == (tag >> 1)
    owner_col = jnp.sum(
        jnp.where(match, (tag & 1).astype(jnp.float32), 0.0), axis=1, keepdims=True
    )
    values = jnp.dot(
        jnp.where(match, 1.0, 0.0).astype(jnp.bfloat16),
        in_blocks[...].reshape(span, width),
        preferred_element_type=jnp.float32,
    )
    mods = mods_ref[...]
    first = owner_col < 0.5
    shift = jnp.where(first, mods[0:1, :width], mods[1:2, :width])
    scale = jnp.where(first, mods[0:1, width : 2 * width], mods[1:2, width : 2 * width])
    hidden = (layer_norm(values) * (1.0 + scale) + shift).astype(jnp.bfloat16)
    mine = pl.ds(pl.multiple_of(u * rows, rows), rows)
    for part in range(groups):
        hidden_all[part, mine, :] = hidden[:, part * depth : (part + 1) * depth]
    counts_all[u] = jnp.broadcast_to(
        jnp.sum(jnp.where(first, 1.0, 0.0), axis=0, keepdims=True), counts_all.shape[1:]
    )

    def hidden_copy(k):
        return pltpu.make_async_remote_copy(
            src_ref=hidden_all.at[:, mine, :],
            dst_ref=hidden_all.at[:, mine, :],
            send_sem=hid_send.at[k],
            recv_sem=hid_recv.at[k],
            device_id=(g, (u + k) % lanes),
            device_id_type=MESH,
        )

    def count_copy(k):
        return pltpu.make_async_remote_copy(
            src_ref=counts_all.at[u],
            dst_ref=counts_all.at[u],
            send_sem=cnt_send.at[k],
            recv_sem=cnt_recv.at[k],
            device_id=(g, (u + k) % lanes),
            device_id_type=MESH,
        )

    for k in range(1, lanes):
        hidden_copy(k).start()
        count_copy(k).start()

    for head in range(heads):
        raw = text_ref[:, 2 * head * HD : (2 * head + 1) * HD].astype(jnp.float32)
        text_keys[head] = rms_scale(raw, gains_ref[1:2, :]).astype(jnp.bfloat16)
    own_copy.wait()

    def pass_on(step):
        for chunk in range(CHUNKS):
            for way in range(2):
                ring_copy(way, chunk, step).wait()

                @pl.when(step < groups - 2)
                def _():
                    ring_copy(way, chunk, step + 1).start()

    def add_block(step):
        left = group_at((position + groups - step) % groups)
        right = group_at((position + step) % groups)
        acc_ref[:, :half] += jnp.dot(
            hidden_all[left], weight_all[left, :, :half], preferred_element_type=jnp.float32
        )
        acc_ref[:, half:] += jnp.dot(
            hidden_all[right], weight_all[right, :, half:], preferred_element_type=jnp.float32
        )

    early = groups // 2 - 1

    def forward_only(step, carry):
        pass_on(step)
        return carry

    lax.fori_loop(0, early, forward_only, 0)
    acc_ref[...] = jnp.zeros_like(acc_ref)
    for k in range(1, lanes):
        hidden_copy(k).wait()
        count_copy(k).wait()

    def held(step, carry):
        add_block(step)
        return carry

    def arriving(step, carry):
        pass_on(step)
        add_block(step + 1)
        return carry

    lax.fori_loop(0, early + 1, held, 0)
    lax.fori_loop(early, groups - 2, arriving, 0)

    reach = (groups // 2, (groups - 1) // 2)

    def out_owner(way, step):
        if way == 0:
            return group_at((position + groups - step) % groups)
        return group_at((position + step) % groups)

    def out_copy(way, chunk, step):
        place = out_weight_all.at[
            out_owner(way, step), pl.ds(chunk * out_piece, out_piece), :
        ]
        return pltpu.make_async_remote_copy(
            src_ref=place,
            dst_ref=place,
            send_sem=out_send.at[way, chunk, step],
            recv_sem=out_recv.at[way, chunk, step],
            device_id=((ahead, behind)[way], u),
            device_id_type=MESH,
        )

    def pass_on_out(step):
        for chunk in range(CHUNKS):
            for way in range(2):
                if step < reach[way]:
                    out_copy(way, chunk, step).wait()
                    if step + 1 < reach[way]:
                        out_copy(way, chunk, step + 1).start()

    for chunk in range(CHUNKS):
        for way in range(2):
            if reach[way] > 0:
                out_copy(way, chunk, 0).start()
    arriving(groups - 2, 0)

    first_tokens = jnp.sum(counts_all[...], axis=0)[0:1, 0:1].astype(jnp.int32)
    key_owner = (
        lax.broadcasted_iota(jnp.int32, (1, count), 1) >= first_tokens
    ).astype(jnp.int32)
    text_code = text_code_ref[0:1, :]
    tile = count // 2
    scaling = HD ** (-0.5)
    dims = (((1,), (1,)), ((), ()))
    pieces = 2 * heads
    done = 0
    for head in range(heads):
        base = 3 * head * HD
        keys = rms_scale(acc_ref[:, base + HD : base + 2 * HD], gains_ref[1:2, :]).astype(
            jnp.bfloat16
        )
        vals = acc_ref[:, base + 2 * HD : base + 3 * HD].astype(jnp.bfloat16)
        text_vals = text_ref[:, (2 * head + 1) * HD : (2 * head + 2) * HD]
        for part in range(2):
            at = part * tile
            query = rms_scale(acc_ref[at : at + tile, base : base + HD], gains_ref[0:1, :]).astype(
                jnp.bfloat16
            )
            query_owner = (
                at + lax.broadcasted_iota(jnp.int32, (tile, 1), 0) >= first_tokens
            ).astype(jnp.int32)
            scores = lax.dot_general(query, keys, dims, preferred_element_type=jnp.float32)
            near = jnp.where(query_owner == key_owner, jnp.exp(scores * scaling), 0.0)
            scores = lax.dot_general(
                query, text_keys[head], dims, preferred_element_type=jnp.float32
            )
            far = jnp.where(query_owner == text_code, jnp.exp(scores * scaling), 0.0)
            total = jnp.sum(near, axis=1, keepdims=True) + jnp.sum(far, axis=1, keepdims=True)
            summed = jnp.dot(
                near.astype(jnp.bfloat16), vals, preferred_element_type=jnp.float32
            ) + jnp.dot(far.astype(jnp.bfloat16), text_vals, preferred_element_type=jnp.float32)
            mixed_ref[at : at + tile, head * HD : (head + 1) * HD] = (summed / total).astype(
                jnp.bfloat16
            )
            until = (2 * head + part + 1) * (reach[0] // 2) // pieces
            while done < until:
                pass_on_out(done)
                done += 1

    order = sorted(range(1, lanes), key=lambda k: abs(k - lanes // 2))
    slots = [(0, 0)]
    for step in range(1, reach[0] + 1):
        slots += [(way, step) for way in range(2) if step <= reach[way]]

    def sum_copy(k, index):
        way, step = slots[index]
        owner = out_owner(way, step)
        return pltpu.make_async_remote_copy(
            src_ref=sending.at[k - 1, owner],
            dst_ref=landing.at[k - 1, owner],
            send_sem=sum_send.at[k - 1, index],
            recv_sem=sum_recv.at[k - 1, index],
            device_id=(g, (u + k) % lanes),
            device_id_type=MESH,
        )

    for index, (way, step) in enumerate(slots):
        while done < step:
            pass_on_out(done)
            done += 1
        owner = out_owner(way, step)
        block = out_weight_all[owner]
        for k in order:
            peer = pl.multiple_of((u + k) % lanes * rows, rows)
            sending[k - 1, owner] = jnp.dot(
                mixed_ref[pl.ds(peer, rows), :], block, preferred_element_type=jnp.float32
            ).astype(jnp.bfloat16)
            sum_copy(k, index).start()
        own_sum[owner] = jnp.dot(mixed_ref[mine, :], block, preferred_element_type=jnp.float32)
    for index in range(len(slots)):
        for k in order:
            sum_copy(k, index).wait()
    gate = jnp.where(first, mods[0:1, 2 * width :], mods[1:2, 2 * width :])
    for part in range(groups):
        sum_here = own_sum[part]
        for k in order:
            sum_here += landing[k - 1, part].astype(jnp.float32)
        here = slice(part * depth, (part + 1) * depth)
        out_ref[:, here] = (gate[:, here] * sum_here).astype(out_ref.dtype)


def sublayer(tokens, place, tags, mods, qkv_weight, gains, text, text_code, out_weight, pad):
    groups = lax.axis_size("grp")
    lanes = lax.axis_size("uly")
    rows, width = tokens.shape
    depth, columns = qkv_weight.shape
    heads = columns // (3 * HD)
    share = out_weight.shape[0] // lanes
    out_columns = out_weight.shape[1]
    count = rows * lanes
    vmem = pl.BlockSpec(memory_space=pltpu.VMEM)
    dma = pltpu.SemaphoreType.DMA
    return pl.pallas_call(
        functools.partial(fused_kernel, groups, lanes, pad),
        out_shape=jax.ShapeDtypeStruct((rows, width), jnp.bfloat16),
        in_specs=[vmem] * 8 + [pl.BlockSpec(memory_space=pl.ANY)],
        out_specs=vmem,
        scratch_shapes=[
            pltpu.VMEM((count, columns), jnp.float32),
            pltpu.VMEM((groups, share, out_columns), jnp.bfloat16),
            pltpu.VMEM((heads, text.shape[0], HD), jnp.bfloat16),
            pltpu.VMEM((count, heads * HD), jnp.bfloat16),
            pltpu.VMEM((groups, rows, out_columns), jnp.float32),
            pltpu.VMEM((lanes - 1, groups, rows, out_columns), jnp.bfloat16),
            pltpu.VMEM((lanes - 1, groups, rows, out_columns), jnp.bfloat16),
            pltpu.VMEM((groups, pad, width), jnp.bfloat16),
            pltpu.VMEM((groups, pad, width), jnp.bfloat16),
            pltpu.VMEM((groups, 8, groups * pad), jnp.int32),
            pltpu.VMEM((groups, count, depth), jnp.bfloat16),
            pltpu.VMEM((groups, depth, columns), jnp.bfloat16),
            pltpu.VMEM((lanes, 8, 128), jnp.float32),
            dma((groups,)),
            dma((groups,)),
            dma((groups,)),
            dma((groups,)),
            dma((lanes,)),
            dma((lanes,)),
            dma((lanes,)),
            dma((lanes,)),
            dma((2, CHUNKS, groups)),
            dma((2, CHUNKS, groups)),
            dma((2, CHUNKS, groups)),
            dma((2, CHUNKS, groups)),
            dma((lanes, groups)),
            dma((lanes, groups)),
            dma,
        ],
        compiler_params=pltpu.CompilerParams(
            collective_id=0, has_side_effects=True, vmem_limit_bytes=58 * 1024 * 1024
        ),
    )(tokens, place, tags, mods, qkv_weight, gains, text, text_code, out_weight)


def body(
    tokens,
    block_image,
    dest_slot,
    timestep,
    txt_len,
    mod_weight,
    qkv_weight,
    q_gain,
    k_gain,
    text_kv,
    out_weight,
):
    groups = lax.axis_size("grp")
    rows, width = tokens.shape
    blocks = block_image.shape[0]
    capacity = (blocks + groups - 1) // groups
    pad = (capacity * BLK + 15) // 16 * 16
    span = groups * pad
    g = lax.axis_index("grp")
    target = block_image // IMG_GRP
    own_image = block_image % IMG_GRP
    index = jnp.arange(blocks, dtype=jnp.int32)
    before = jnp.sum(
        ((target[:, None] == target[None, :]) & (index[None, :] < index[:, None])).astype(jnp.int32),
        axis=1,
    )
    row = jnp.arange(BLK, dtype=jnp.int32)
    place = ((target * pad + before * BLK)[:, None] + row[None, :]).reshape(rows)
    code = ((dest_slot[:, None] * BLK + row[None, :]) * 2 + own_image[:, None]).reshape(rows)
    hits = place[None, :] == jnp.arange(span, dtype=jnp.int32)[:, None]
    codes = (jnp.sum(jnp.where(hits, code[None, :] + 1, 0), axis=1) - 1).reshape(groups, pad)
    own_lane = jnp.arange(span, dtype=jnp.int32) // pad == g
    tags = jnp.where(own_lane[None, :], jnp.tile(codes, (1, groups)), -1)
    tags = jnp.broadcast_to(tags[:, None, :], (groups, 8, span))
    places = jnp.broadcast_to(place[None, :], (8, rows))

    mods = modulation(timestep, mod_weight)
    text = text_kv.reshape(IMG_GRP * TXT, text_kv.shape[2])
    live = jnp.arange(TXT, dtype=jnp.int32)[None, :] < txt_len[:, None]
    text_code = jnp.where(live, jnp.arange(IMG_GRP, dtype=jnp.int32)[:, None], -1)
    text_code = jnp.broadcast_to(text_code.reshape(1, IMG_GRP * TXT), (8, IMG_GRP * TXT))
    gains = jnp.stack([q_gain, k_gain])
    return sublayer(
        tokens, places, tags, mods, qkv_weight, gains, text, text_code, out_weight, pad
    )


def solution(mesh):
    return jax.shard_map(
        body,
        mesh=mesh,
        in_specs=(
            P(("grp", "uly"), None),
            P(("grp", "uly")),
            P(("grp", "uly")),
            P("grp"),
            P("grp"),
            P(),
            P("grp", "uly"),
            P(),
            P(),
            P("grp", None, "uly"),
            P(None, "grp"),
        ),
        out_specs=P(("grp", "uly"), None),
        check_vma=False,
    )
```
